32 devices in a mesh: groups: 2 (over y), grid: 8 (over z, x), depth: 2 (over core).
Axes of the slice: x: 2, y: 2, z: 4, core: 2. Of those that a mesh axis runs over, the one named last changes fastest.
Arguments:
- band_held: bfloat16 [2048, 4096], P('groups', 'grid'), parts along dimension 0, may hold values from -6 to 6
- inner_tiles: bfloat16 [6144, 4096], P(('groups', 'depth'), 'grid'), parts along dimension 0, may hold values from -0.109375 to 0.109375
- band_mask: int32 [4, 8], P('groups'), parts along dimension 0, may hold values 0 or 1
- inner_mask: int32 [12, 8], P(('groups', 'depth'), 'grid'), parts along dimension 0, may hold values 0 or 1
- held_col: int32 [16], P('groups'), parts along dimension 0, may hold values from 0 to 7, each once
Outputs:
- product: bfloat16 [2048, 4096], P(('groups', 'depth'), 'grid'), parts along dimension 0
The draws below stay inside these ranges and needn't reach their ends.
There are 2 independent parts, one for each index of `groups`. The reference program is written for one: setup_inputs(seed, part) draws one part's arguments, and reference() takes and returns one part's arrays. A program takes and returns all parts, laid end to end along the dimension named above; each array names one. Nothing has to cross between parts.
Inputs may be any that keep to these rules, and one draw needn't show every extreme that they name: held_col holds every tile column once.
All inputs are finite; a program needn't handle non-finite values. No bound on the sum of `inner_mask` on one device may be relied on, other than what follows from the above.
Results may differ from the reference program's by a relative error of at most 0.001.
Values may be sent and summed in bfloat16 or wider, within the bound.
No kernel may reach another device: no remote copies, remote signals or barrier semaphores. Data moves between devices by JAX's collectives and lax.ppermute only.
A program may use at most 64 MiB of HBM per device.

```python
import jax
import jax.numpy as jnp
from jax import lax

TILE = 512
BAND = 2
OFFS = 6
NT = 8


def plant(values, stream_key, smallest, top_value):
    extent = values.shape
    place = [jax.random.randint(jax.random.fold_in(stream_key, axis), (), 0, extent[axis]) for axis in range(len(extent))]
    values = values.at[tuple(place)].set(smallest)
    longest = extent.index(max(extent))
    place[longest] = (place[longest] + 1) % extent[longest]
    return values.at[tuple(place)].set(top_value)


def steps_of(own_key, shape, shards, low, top_value):
    def one(position, blocks):
        draws = jax.random.uniform(jax.random.fold_in(jax.random.fold_in(own_key, 6), position), (blocks,), jnp.float32, low / len(shards), top_value / len(shards))
        return jnp.repeat(jnp.exp(draws), shape[position] // blocks).reshape((-1,) + (1,) * (len(shape) - position - 1))

    factor_of = one(*shards[0])
    for cut in shards[1:]:
        factor_of = factor_of * one(*cut)
    return factor_of


def normal_values(key, dims, scale, limit, shards=(), kind=jnp.bfloat16):
    level = steps_of(key, dims, shards, -0.22, 0.18) if shards else 1.0
    result = jax.random.normal(key, dims, jnp.float32) * scale * level
    return jnp.minimum(jnp.maximum(result, -limit), limit).astype(kind)


def setup_inputs(seed: int = 0, part: int = 0) -> dict:
    key_list = jax.random.split(jax.random.key(seed), 6)
    part_keys = jax.random.split(jax.random.fold_in(key_list[5], part), 6)
    band_held = normal_values(part_keys[0], (BAND * TILE, NT * TILE), 1.0, 6.0, ((1, 8),))
    inner_tiles = normal_values(part_keys[1], (OFFS * TILE, NT * TILE), (OFFS * TILE) ** -0.5, 0.109375, ((0, 2), (1, 8)))
    band_mask = plant((jax.random.randint(part_keys[2], (BAND, NT), 0, 4) < 3).astype(jnp.int32), jax.random.fold_in(part_keys[2], 1), 0, 1)
    inner_mask = plant((jax.random.randint(part_keys[3], (OFFS, NT), 0, 2) < 1).astype(jnp.int32), jax.random.fold_in(part_keys[3], 1), 0, 1)
    held_col = jax.random.permutation(part_keys[4], NT).astype(jnp.int32)
    return {"band_held": band_held, "inner_tiles": inner_tiles, "band_mask": band_mask, "inner_mask": inner_mask, "held_col": held_col}


def reference(band_held, inner_tiles, band_mask, inner_mask, held_col):
    half_window = OFFS // 2
    row_count = BAND * TILE
    col_order = jnp.arange(NT, dtype=jnp.int32)
    inverse = jnp.sum(jnp.where(held_col[None, :] == col_order[:, None], col_order[None, :], 0), axis=1).astype(jnp.int32)
    strips = band_held.reshape(row_count, NT, TILE)
    ordered = jnp.take(strips, inverse, axis=1)
    padded = jnp.pad(ordered, ((0, 0), (half_window, half_window), (0, 0)))
    mask_pad = jnp.pad(band_mask, ((0, 0), (half_window, half_window)))
    tile_grid = inner_tiles.reshape(OFFS, TILE, NT, TILE)

    def one_column(col_index):
        window = lax.dynamic_slice_in_dim(padded, col_index, OFFS, 1)
        keep_flags = lax.dynamic_slice_in_dim(mask_pad, col_index, OFFS, 1)
        inner_flags = lax.dynamic_index_in_dim(inner_mask, col_index, 1, keepdims=False)
        keep_flags = keep_flags * inner_flags[None, :]
        keep_rows = jnp.repeat(keep_flags, TILE, axis=0).astype(jnp.float32)
        right_tiles = lax.dynamic_index_in_dim(tile_grid, col_index, 2, keepdims=False)
        masked = window.astype(jnp.float32) * keep_rows[:, :, None]
        summed = jnp.einsum("rot,otc->rc", masked, right_tiles.astype(jnp.float32))
        return summed.astype(jnp.bfloat16)

    blocks = lax.map(one_column, col_order)
    return jnp.transpose(blocks, (1, 0, 2)).reshape(row_count, NT * TILE)
```

```python
import functools

import jax
import jax.numpy as jnp
from jax import lax
from jax.experimental import pallas as pl
from jax.experimental.pallas import tpu as pltpu
from jax.sharding import PartitionSpec as P


def exchange_columns(band_held, inner_tiles, band_mask, inner_mask, held_col):
    grid_size = lax.axis_size("grid")
    tile_size = band_held.shape[1]
    band_count = band_mask.shape[0]
    local_offsets = inner_mask.shape[0]
    depth_index = lax.axis_index("depth")
    column = lax.axis_index("grid")
    first_offset = depth_index * local_offsets
    right_flags = inner_mask[:, 0]
    row_count = band_count * tile_size
    col_order = jnp.arange(grid_size, dtype=jnp.int32)
    inverse = jnp.sum(
        jnp.where(held_col[None, :] == col_order[:, None], col_order[None, :], 0), axis=1
    )
    pieces = lax.all_to_all(
        band_held.reshape(row_count, 1, tile_size), "grid", split_axis=0, concat_axis=1, tiled=True
    )
    ordered = jnp.take(pieces, inverse, axis=1)
    padded = jnp.pad(ordered, ((0, 0), (local_offsets, local_offsets), (0, 0)))
    windows = jnp.stack(
        [
            lax.dynamic_slice_in_dim(padded, first_offset + offset, grid_size, 1)
            for offset in range(local_offsets)
        ],
        axis=2,
    )
    arrived = lax.all_to_all(windows, "grid", split_axis=1, concat_axis=0, tiled=True)
    arrived = arrived.reshape(row_count, local_offsets, tile_size)
    flags_pad = jnp.pad(band_mask, ((0, 0), (local_offsets, local_offsets)))
    keep_flags = (
        lax.dynamic_slice_in_dim(flags_pad, column + first_offset, local_offsets, 1)
        * right_flags[None, :]
    )
    keep_rows = jnp.repeat(keep_flags, tile_size, axis=0).astype(jnp.float32)
    summed = jnp.zeros((row_count, tile_size), jnp.float32)
    for offset in range(local_offsets):
        right_block = inner_tiles[offset * tile_size : (offset + 1) * tile_size]
        summed = (
            summed
            + jnp.dot(arrived[:, offset, :], right_block, preferred_element_type=jnp.float32)
            * keep_rows[:, offset : offset + 1]
        )
    summed = lax.psum_scatter(summed, "depth", scatter_dimension=0, tiled=True)
    return summed.astype(jnp.bfloat16)


def add_products(places, slots, flags, pieces, inner, total):
    for (source, row), piece in zip(places, pieces):
        rows = pl.ds(row, piece.shape[0])

        @pl.when(flags[source] != 0)
        def _():
            total[rows, :] += jnp.dot(
                piece[...], inner[slots[source]], preferred_element_type=jnp.float32
            )


def early_kernel(places, slots, flags, inner, *refs):
    total = refs[-1]
    total[...] = jnp.zeros_like(total)
    add_products(places, slots, flags, refs[:-1], inner, total)


def late_kernel(places, slots, flags, inner, before, *refs):
    *pieces, out, total = refs
    total[...] = before[...]
    add_products(places, slots, flags, pieces, inner, total)
    out[...] = total[...].astype(out.dtype)


def multiply(kernel, places, slots, flags, arrays, out_shape, scratch):
    size = arrays[0].shape[-1]
    smem, vmem = pl.BlockSpec(memory_space=pltpu.SMEM), pl.BlockSpec(memory_space=pltpu.VMEM)
    return pl.pallas_call(
        functools.partial(kernel, places),
        out_shape=out_shape,
        in_specs=[smem, smem] + [vmem] * len(arrays),
        out_specs=vmem,
        scratch_shapes=scratch,
        compiler_params=pltpu.CompilerParams(vmem_limit_bytes=40 * 2**20),
        cost_estimate=pl.CostEstimate(
            flops=len(places) * size**3,
            bytes_accessed=sum(a.size * a.dtype.itemsize for a in arrays),
            transcendentals=0,
        ),
    )(slots, flags, *arrays)


def gather_columns(band_held, inner_tiles, band_mask, inner_mask, held_col):
    grid_size = lax.axis_size("grid")
    size = band_held.shape[1]
    local_offsets = inner_mask.shape[0]
    halves = lax.axis_size("depth")
    depth_index = lax.axis_index("depth")
    column = lax.axis_index("grid")
    half = size // 2

    order = list(range(0, grid_size, 2)) + list(range(1, grid_size, 2))[::-1]
    onward = [(order[i], order[(i + 1) % grid_size]) for i in range(grid_size)]
    backward = [(b, a) for a, b in onward]
    position_of = [order.index(g) for g in range(grid_size)]

    own = lax.dynamic_slice_in_dim(band_held, depth_index * size, size, 0)
    first = [own[:half], own[half:]]
    pieces = {(0, 0): first[0], (0, 1): first[1]}
    right, left = list(first), list(first)
    steps = (grid_size - 1) // 2
    for step in range(1, steps + 1):
        for h in (0, 1):
            right[h] = lax.ppermute(right[h], "grid", onward)
            left[1 - h] = lax.ppermute(left[1 - h], "grid", backward)
            pieces[(grid_size - step, h)] = right[h]
            pieces[(step, 1 - h)] = left[1 - h]
    last = {}
    if grid_size % 2 == 0:
        last[(steps + 1, 0)] = lax.ppermute(right[0], "grid", onward)
        last[(steps + 1, 1)] = lax.ppermute(left[1], "grid", backward)

    masked = inner_tiles.reshape(local_offsets, size, size) * inner_mask[:, :, None].astype(
        inner_tiles.dtype
    )
    swapped = lax.ppermute(masked, "depth", [(0, 1), (1, 0)])
    inner = jnp.concatenate([masked, swapped], axis=0)

    position = jnp.asarray(position_of, jnp.int32)[column]
    sources = jnp.asarray(order, jnp.int32)[
        (position + jnp.arange(grid_size, dtype=jnp.int32)) % grid_size
    ]
    true_column = held_col[sources]
    offset = true_column - column + local_offsets * halves // 2
    inside = (offset >= 0) & (offset < local_offsets * halves)
    offset = jnp.clip(offset, 0, local_offsets * halves - 1)
    band_row = lax.dynamic_index_in_dim(band_mask, depth_index, 0, keepdims=False)
    flags = jnp.where(inside, band_row[true_column], 0).astype(jnp.int32)
    slots = (
        jnp.where(offset // local_offsets == depth_index, 0, local_offsets)
        + offset % local_offsets
    ).astype(jnp.int32)

    def placed(items):
        return [(source, h * half) for source, h in items]

    total_shape = jax.ShapeDtypeStruct((size, size), jnp.float32)
    early = multiply(
        early_kernel, placed(pieces), slots, flags, [inner, *pieces.values()], total_shape, []
    )
    return multiply(
        late_kernel,
        placed(last),
        slots,
        flags,
        [inner, early, *last.values()],
        jax.ShapeDtypeStruct((size, size), band_held.dtype),
        [pltpu.VMEM((size, size), jnp.float32)],
    )


def per_device(band_held, inner_tiles, band_mask, inner_mask, held_col):
    window = inner_mask.shape[0] * lax.axis_size("depth")
    small = lax.axis_size("grid") <= 2 * window
    fits = lax.axis_size("depth") == 2 and band_mask.shape[0] == 2 and lax.axis_size("grid") % 2 == 0
    chosen = gather_columns if small and fits else exchange_columns
    return chosen(band_held, inner_tiles, band_mask, inner_mask, held_col)


def solution(mesh):
    placed = (
        P("groups", "grid"),
        P(("groups", "depth"), "grid"),
        P("groups", None),
        P(("groups", "depth"), "grid"),
        P("groups"),
    )
    return jax.shard_map(
        per_device,
        mesh=mesh,
        in_specs=placed,
        out_specs=P(("groups", "depth"), "grid"),
        check_vma=False,
    )
```

```python
import functools

import jax
import jax.numpy as jnp
from jax import lax
from jax.experimental import pallas as pl
from jax.experimental.pallas import tpu as pltpu
from jax.sharding import PartitionSpec as P


def exchange_columns(band_held, inner_tiles, band_mask, inner_mask, held_col):
    grid_size = lax.axis_size("grid")
    tile_size = band_held.shape[1]
    band_count = band_mask.shape[0]
    local_offsets = inner_mask.shape[0]
    depth_index = lax.axis_index("depth")
    column = lax.axis_index("grid")
    first_offset = depth_index * local_offsets
    right_flags = inner_mask[:, 0]
    row_count = band_count * tile_size
    col_order = jnp.arange(grid_size, dtype=jnp.int32)
    inverse = jnp.sum(
        jnp.where(held_col[None, :] == col_order[:, None], col_order[None, :], 0), axis=1
    )
    pieces = lax.all_to_all(
        band_held.reshape(row_count, 1, tile_size), "grid", split_axis=0, concat_axis=1, tiled=True
    )
    ordered = jnp.take(pieces, inverse, axis=1)
    padded = jnp.pad(ordered, ((0, 0), (local_offsets, local_offsets), (0, 0)))
    windows = jnp.stack(
        [
            lax.dynamic_slice_in_dim(padded, first_offset + offset, grid_size, 1)
            for offset in range(local_offsets)
        ],
        axis=2,
    )
    arrived = lax.all_to_all(windows, "grid", split_axis=1, concat_axis=0, tiled=True)
    arrived = arrived.reshape(row_count, local_offsets, tile_size)
    flags_pad = jnp.pad(band_mask, ((0, 0), (local_offsets, local_offsets)))
    keep_flags = (
        lax.dynamic_slice_in_dim(flags_pad, column + first_offset, local_offsets, 1)
        * right_flags[None, :]
    )
    keep_rows = jnp.repeat(keep_flags, tile_size, axis=0).astype(jnp.float32)
    summed = jnp.zeros((row_count, tile_size), jnp.float32)
    for offset in range(local_offsets):
        right_block = inner_tiles[offset * tile_size : (offset + 1) * tile_size]
        summed = (
            summed
            + jnp.dot(arrived[:, offset, :], right_block, preferred_element_type=jnp.float32)
            * keep_rows[:, offset : offset + 1]
        )
    summed = lax.psum_scatter(summed, "depth", scatter_dimension=0, tiled=True)
    return summed.astype(jnp.bfloat16)


def add_products(places, slots, flags, pieces, inner, total):
    for (source, row), piece in zip(places, pieces):
        rows = pl.ds(row, piece.shape[0])

        @pl.when(flags[source] != 0)
        def _():
            total[rows, :] += jnp.dot(
                piece[...], inner[slots[source]], preferred_element_type=jnp.float32
            )


def early_kernel(places, slots, flags, inner, *refs):
    total = refs[-1]
    total[...] = jnp.zeros_like(total)
    add_products(places, slots, flags, refs[:-1], inner, total)


def late_kernel(places, slots, flags, inner, before, *refs):
    *pieces, out, total = refs
    total[...] = before[...]
    add_products(places, slots, flags, pieces, inner, total)
    out[...] = total[...].astype(out.dtype)


def multiply(kernel, places, slots, flags, arrays, out_shape, scratch):
    size = arrays[0].shape[-1]
    smem, vmem = pl.BlockSpec(memory_space=pltpu.SMEM), pl.BlockSpec(memory_space=pltpu.VMEM)
    return pl.pallas_call(
        functools.partial(kernel, places),
        out_shape=out_shape,
        in_specs=[smem, smem] + [vmem] * len(arrays),
        out_specs=vmem,
        scratch_shapes=scratch,
        compiler_params=pltpu.CompilerParams(vmem_limit_bytes=40 * 2**20),
        cost_estimate=pl.CostEstimate(
            flops=len(places) * size**3,
            bytes_accessed=sum(a.size * a.dtype.itemsize for a in arrays),
            transcendentals=0,
        ),
    )(slots, flags, *arrays)


def gather_columns(band_held, inner_tiles, band_mask, inner_mask, held_col):
    grid_size = lax.axis_size("grid")
    size = band_held.shape[1]
    local_offsets = inner_mask.shape[0]
    halves = lax.axis_size("depth")
    depth_index = lax.axis_index("depth")
    column = lax.axis_index("grid")
    half = size // 2

    order = list(range(0, grid_size, 2)) + list(range(1, grid_size, 2))[::-1]
    onward = [(order[i], order[(i + 1) % grid_size]) for i in range(grid_size)]
    backward = [(b, a) for a, b in onward]
    position_of = [order.index(g) for g in range(grid_size)]

    own = lax.dynamic_slice_in_dim(band_held, depth_index * size, size, 0)
    first = [own[:half], own[half:]]
    pieces = {(0, 0): first[0], (0, 1): first[1]}
    right, left = list(first), list(first)
    steps = (grid_size - 1) // 2
    for step in range(1, steps + 1):
        for h in (0, 1):
            right[h] = lax.ppermute(right[h], "grid", onward)
            left[1 - h] = lax.ppermute(left[1 - h], "grid", backward)
            pieces[(grid_size - step, h)] = right[h]
            pieces[(step, 1 - h)] = left[1 - h]
    last = {}
    if grid_size % 2 == 0:
        last[(steps + 1, 0)] = lax.ppermute(right[0], "grid", onward)
        last[(steps + 1, 1)] = lax.ppermute(left[1], "grid", backward)

    swapped = lax.ppermute(inner_tiles, "depth", [(0, 1), (1, 0)])
    inner = jnp.concatenate([inner_tiles, swapped], axis=0).reshape(-1, size, size)
    inner_mask, _ = lax.optimization_barrier((inner_mask, pieces[(grid_size - 1, 0)]))
    tile_flags = jnp.concatenate(
        [inner_mask, lax.ppermute(inner_mask, "depth", [(0, 1), (1, 0)])], axis=0
    )[:, 0]

    position = jnp.asarray(position_of, jnp.int32)[column]
    sources = jnp.asarray(order, jnp.int32)[
        (position + jnp.arange(grid_size, dtype=jnp.int32)) % grid_size
    ]
    true_column = held_col[sources]
    offset = true_column - column + local_offsets * halves // 2
    inside = (offset >= 0) & (offset < local_offsets * halves)
    offset = jnp.clip(offset, 0, local_offsets * halves - 1)
    band_row = lax.dynamic_index_in_dim(band_mask, depth_index, 0, keepdims=False)
    flags = jnp.where(inside, band_row[true_column], 0).astype(jnp.int32)
    slots = (
        jnp.where(offset // local_offsets == depth_index, 0, local_offsets)
        + offset % local_offsets
    ).astype(jnp.int32)

    flags = flags * tile_flags[slots]

    def placed(items):
        return [(source, h * half) for source, h in items]

    total_shape = jax.ShapeDtypeStruct((size, size), jnp.float32)
    early = multiply(
        early_kernel, placed(pieces), slots, flags, [inner, *pieces.values()], total_shape, []
    )
    return multiply(
        late_kernel,
        [(0, h * half) for _, h in last],
        jnp.zeros((1,), jnp.int32),
        flags[steps + 1 :][:1],
        [
            lax.dynamic_slice_in_dim(inner, slots[steps + 1], 1, 0),
            early,
            *last.values(),
        ],
        jax.ShapeDtypeStruct((size, size), band_held.dtype),
        [pltpu.VMEM((size, size), jnp.float32)],
    )


def per_device(band_held, inner_tiles, band_mask, inner_mask, held_col):
    window = inner_mask.shape[0] * lax.axis_size("depth")
    small = lax.axis_size("grid") <= 2 * window
    fits = lax.axis_size("depth") == 2 and band_mask.shape[0] == 2 and lax.axis_size("grid") % 2 == 0
    chosen = gather_columns if small and fits else exchange_columns
    return chosen(band_held, inner_tiles, band_mask, inner_mask, held_col)


def solution(mesh):
    placed = (
        P("groups", "grid"),
        P(("groups", "depth"), "grid"),
        P("groups", None),
        P(("groups", "depth"), "grid"),
        P("groups"),
    )
    return jax.shard_map(
        per_device,
        mesh=mesh,
        in_specs=placed,
        out_specs=P(("groups", "depth"), "grid"),
        check_vma=False,
    )
```

```python
import functools

import jax
import jax.numpy as jnp
from jax import lax
from jax.experimental import pallas as pl
from jax.experimental.pallas import tpu as pltpu
from jax.sharding import PartitionSpec as P


def exchange_columns(band_held, inner_tiles, band_mask, inner_mask, held_col):
    grid_size = lax.axis_size("grid")
    tile_size = band_held.shape[1]
    band_count = band_mask.shape[0]
    local_offsets = inner_mask.shape[0]
    depth_index = lax.axis_index("depth")
    column = lax.axis_index("grid")
    first_offset = depth_index * local_offsets
    right_flags = inner_mask[:, 0]
    row_count = band_count * tile_size
    col_order = jnp.arange(grid_size, dtype=jnp.int32)
    inverse = jnp.sum(
        jnp.where(held_col[None, :] == col_order[:, None], col_order[None, :], 0), axis=1
    )
    pieces = lax.all_to_all(
        band_held.reshape(row_count, 1, tile_size), "grid", split_axis=0, concat_axis=1, tiled=True
    )
    ordered = jnp.take(pieces, inverse, axis=1)
    padded = jnp.pad(ordered, ((0, 0), (local_offsets, local_offsets), (0, 0)))
    windows = jnp.stack(
        [
            lax.dynamic_slice_in_dim(padded, first_offset + offset, grid_size, 1)
            for offset in range(local_offsets)
        ],
        axis=2,
    )
    arrived = lax.all_to_all(windows, "grid", split_axis=1, concat_axis=0, tiled=True)
    arrived = arrived.reshape(row_count, local_offsets, tile_size)
    flags_pad = jnp.pad(band_mask, ((0, 0), (local_offsets, local_offsets)))
    keep_flags = (
        lax.dynamic_slice_in_dim(flags_pad, column + first_offset, local_offsets, 1)
        * right_flags[None, :]
    )
    keep_rows = jnp.repeat(keep_flags, tile_size, axis=0).astype(jnp.float32)
    summed = jnp.zeros((row_count, tile_size), jnp.float32)
    for offset in range(local_offsets):
        right_block = inner_tiles[offset * tile_size : (offset + 1) * tile_size]
        summed = (
            summed
            + jnp.dot(arrived[:, offset, :], right_block, preferred_element_type=jnp.float32)
            * keep_rows[:, offset : offset + 1]
        )
    summed = lax.psum_scatter(summed, "depth", scatter_dimension=0, tiled=True)
    return summed.astype(jnp.bfloat16)


def add_products(places, slots, flags, pieces, inner, total):
    for (source, row), piece in zip(places, pieces):
        rows = pl.ds(row, piece.shape[0])

        @pl.when(flags[source] != 0)
        def _():
            total[rows, :] += jnp.dot(
                piece[...], inner[slots[source]], preferred_element_type=jnp.float32
            )


def early_kernel(places, slots, flags, inner, *refs):
    total = refs[-1]
    total[...] = jnp.zeros_like(total)
    add_products(places, slots, flags, refs[:-1], inner, total)


def late_kernel(places, slots, flags, inner, before, *refs):
    *pieces, out, total = refs
    total[...] = before[...]
    add_products(places, slots, flags, pieces, inner, total)
    out[...] = total[...].astype(out.dtype)


def multiply(kernel, places, slots, flags, arrays, out_shape, scratch):
    size = arrays[0].shape[-1]
    smem, vmem = pl.BlockSpec(memory_space=pltpu.SMEM), pl.BlockSpec(memory_space=pltpu.VMEM)
    return pl.pallas_call(
        functools.partial(kernel, places),
        out_shape=out_shape,
        in_specs=[smem, smem] + [vmem] * len(arrays),
        out_specs=vmem,
        scratch_shapes=scratch,
        compiler_params=pltpu.CompilerParams(vmem_limit_bytes=40 * 2**20),
        cost_estimate=pl.CostEstimate(
            flops=len(places) * size**3,
            bytes_accessed=sum(a.size * a.dtype.itemsize for a in arrays),
            transcendentals=0,
        ),
    )(slots, flags, *arrays)


def gather_columns(band_held, inner_tiles, band_mask, inner_mask, held_col):
    grid_size = lax.axis_size("grid")
    size = band_held.shape[1]
    local_offsets = inner_mask.shape[0]
    halves = lax.axis_size("depth")
    depth_index = lax.axis_index("depth")
    column = lax.axis_index("grid")
    half = size // 2

    order = list(range(0, grid_size, 2)) + list(range(1, grid_size, 2))[::-1]
    onward = [(order[i], order[(i + 1) % grid_size]) for i in range(grid_size)]
    backward = [(b, a) for a, b in onward]
    position_of = [order.index(g) for g in range(grid_size)]

    own = lax.dynamic_slice_in_dim(band_held, depth_index * size, size, 0)
    first = [own[:half], own[half:]]
    pieces = {(0, 0): first[0], (0, 1): first[1]}
    late = lax.optimization_barrier((own[:half], own[half:], inner_mask))
    right, left = [first[0], late[1]], [late[0], first[1]]
    steps = (grid_size - 1) // 2
    for step in range(1, steps + 1):
        for h in (0, 1):
            right[h] = lax.ppermute(right[h], "grid", onward)
            left[1 - h] = lax.ppermute(left[1 - h], "grid", backward)
            pieces[(grid_size - step, h)] = right[h]
            pieces[(step, 1 - h)] = left[1 - h]
    last = {}
    if grid_size % 2 == 0:
        last[(steps + 1, 0)] = lax.ppermute(right[0], "grid", onward)
        last[(steps + 1, 1)] = lax.ppermute(left[1], "grid", backward)

    swapped = lax.ppermute(inner_tiles, "depth", [(0, 1), (1, 0)])
    inner = jnp.concatenate([inner_tiles, swapped], axis=0).reshape(-1, size, size)
    inner_mask, _ = lax.optimization_barrier((inner_mask, pieces[(grid_size - 1, 0)]))
    tile_flags = jnp.concatenate(
        [inner_mask, lax.ppermute(inner_mask, "depth", [(0, 1), (1, 0)])], axis=0
    )[:, 0]

    position = jnp.asarray(position_of, jnp.int32)[column]
    sources = jnp.asarray(order, jnp.int32)[
        (position + jnp.arange(grid_size, dtype=jnp.int32)) % grid_size
    ]
    true_column = held_col[sources]
    offset = true_column - column + local_offsets * halves // 2
    inside = (offset >= 0) & (offset < local_offsets * halves)
    offset = jnp.clip(offset, 0, local_offsets * halves - 1)
    band_row = lax.dynamic_index_in_dim(band_mask, depth_index, 0, keepdims=False)
    flags = jnp.where(inside, band_row[true_column], 0).astype(jnp.int32)
    slots = (
        jnp.where(offset // local_offsets == depth_index, 0, local_offsets)
        + offset % local_offsets
    ).astype(jnp.int32)

    flags = flags * tile_flags[slots]

    def placed(items):
        return [(source, h * half) for source, h in items]

    total_shape = jax.ShapeDtypeStruct((size, size), jnp.float32)
    early = multiply(
        early_kernel, placed(pieces), slots, flags, [inner, *pieces.values()], total_shape, []
    )
    return multiply(
        late_kernel,
        [(0, h * half) for _, h in last],
        jnp.zeros((1,), jnp.int32),
        flags[steps + 1 :][:1],
        [
            lax.dynamic_slice_in_dim(inner, slots[steps + 1], 1, 0),
            early,
            *last.values(),
        ],
        jax.ShapeDtypeStruct((size, size), band_held.dtype),
        [pltpu.VMEM((size, size), jnp.float32)],
    )


def per_device(band_held, inner_tiles, band_mask, inner_mask, held_col):
    window = inner_mask.shape[0] * lax.axis_size("depth")
    small = lax.axis_size("grid") <= 2 * window
    fits = lax.axis_size("depth") == 2 and band_mask.shape[0] == 2 and lax.axis_size("grid") % 2 == 0
    chosen = gather_columns if small and fits else exchange_columns
    return chosen(band_held, inner_tiles, band_mask, inner_mask, held_col)


def solution(mesh):
    placed = (
        P("groups", "grid"),
        P(("groups", "depth"), "grid"),
        P("groups", None),
        P(("groups", "depth"), "grid"),
        P("groups"),
    )
    return jax.shard_map(
        per_device,
        mesh=mesh,
        in_specs=placed,
        out_specs=P(("groups", "depth"), "grid"),
        check_vma=False,
    )
```

```python
import functools

import jax
import jax.numpy as jnp
from jax import lax
from jax.experimental import pallas as pl
from jax.experimental.pallas import tpu as pltpu
from jax.sharding import PartitionSpec as P


def exchange_columns(band_held, inner_tiles, band_mask, inner_mask, held_col):
    grid_size = lax.axis_size("grid")
    tile_size = band_held.shape[1]
    band_count = band_mask.shape[0]
    local_offsets = inner_mask.shape[0]
    depth_index = lax.axis_index("depth")
    column = lax.axis_index("grid")
    first_offset = depth_index * local_offsets
    right_flags = inner_mask[:, 0]
    row_count = band_count * tile_size
    col_order = jnp.arange(grid_size, dtype=jnp.int32)
    inverse = jnp.sum(
        jnp.where(held_col[None, :] == col_order[:, None], col_order[None, :], 0), axis=1
    )
    pieces = lax.all_to_all(
        band_held.reshape(row_count, 1, tile_size), "grid", split_axis=0, concat_axis=1, tiled=True
    )
    ordered = jnp.take(pieces, inverse, axis=1)
    padded = jnp.pad(ordered, ((0, 0), (local_offsets, local_offsets), (0, 0)))
    windows = jnp.stack(
        [
            lax.dynamic_slice_in_dim(padded, first_offset + offset, grid_size, 1)
            for offset in range(local_offsets)
        ],
        axis=2,
    )
    arrived = lax.all_to_all(windows, "grid", split_axis=1, concat_axis=0, tiled=True)
    arrived = arrived.reshape(row_count, local_offsets, tile_size)
    flags_pad = jnp.pad(band_mask, ((0, 0), (local_offsets, local_offsets)))
    keep_flags = (
        lax.dynamic_slice_in_dim(flags_pad, column + first_offset, local_offsets, 1)
        * right_flags[None, :]
    )
    keep_rows = jnp.repeat(keep_flags, tile_size, axis=0).astype(jnp.float32)
    summed = jnp.zeros((row_count, tile_size), jnp.float32)
    for offset in range(local_offsets):
        right_block = inner_tiles[offset * tile_size : (offset + 1) * tile_size]
        summed = (
            summed
            + jnp.dot(arrived[:, offset, :], right_block, preferred_element_type=jnp.float32)
            * keep_rows[:, offset : offset + 1]
        )
    summed = lax.psum_scatter(summed, "depth", scatter_dimension=0, tiled=True)
    return summed.astype(jnp.bfloat16)


def add_products(places, slots, flags, pieces, inner, total):
    for (source, row), piece in zip(places, pieces):
        rows = pl.ds(row, piece.shape[0])

        @pl.when(flags[source] != 0)
        def _():
            total[rows, :] += jnp.dot(
                piece[...], inner[slots[source]], preferred_element_type=jnp.float32
            )


def early_kernel(places, slots, flags, inner, *refs):
    total = refs[-1]
    total[...] = jnp.zeros_like(total)
    add_products(places, slots, flags, refs[:-1], inner, total)


def late_kernel(tile, before, *refs):
    *pieces, out, held, sems = refs
    copies = []
    start = 0
    for h, piece in enumerate(pieces):
        rows = pl.ds(start, piece.shape[0])
        start += piece.shape[0]
        product = jnp.dot(piece[...], tile[...], preferred_element_type=jnp.float32)
        held[rows, :] = (before[rows, :] + product).astype(out.dtype)
        copies.append(pltpu.make_async_copy(held.at[rows], out.at[rows], sems.at[h]))
        copies[-1].start()
    for copy in copies:
        copy.wait()


def multiply(kernel, places, slots, flags, arrays, out_shape, scratch):
    size = arrays[0].shape[-1]
    smem, vmem = pl.BlockSpec(memory_space=pltpu.SMEM), pl.BlockSpec(memory_space=pltpu.VMEM)
    return pl.pallas_call(
        functools.partial(kernel, places),
        out_shape=out_shape,
        in_specs=[smem, smem] + [vmem] * len(arrays),
        out_specs=vmem,
        scratch_shapes=scratch,
        compiler_params=pltpu.CompilerParams(vmem_limit_bytes=40 * 2**20),
        cost_estimate=pl.CostEstimate(
            flops=len(places) * size**3,
            bytes_accessed=sum(a.size * a.dtype.itemsize for a in arrays),
            transcendentals=0,
        ),
    )(slots, flags, *arrays)


def gather_columns(band_held, inner_tiles, band_mask, inner_mask, held_col):
    grid_size = lax.axis_size("grid")
    size = band_held.shape[1]
    local_offsets = inner_mask.shape[0]
    halves = lax.axis_size("depth")
    depth_index = lax.axis_index("depth")
    column = lax.axis_index("grid")
    half = (size * 9 // 16) // 16 * 16

    order = list(range(0, grid_size, 2)) + list(range(1, grid_size, 2))[::-1]
    onward = [(order[i], order[(i + 1) % grid_size]) for i in range(grid_size)]
    backward = [(b, a) for a, b in onward]
    position_of = [order.index(g) for g in range(grid_size)]

    begin = depth_index * size
    again, _ = lax.optimization_barrier((band_held, inner_mask))
    first = [
        lax.dynamic_slice_in_dim(band_held, begin, half, 0),
        lax.dynamic_slice_in_dim(again, begin + half, size - half, 0),
    ]
    pieces = {(0, 0): first[0], (0, 1): first[1]}
    late = lax.optimization_barrier((*first, inner_mask))
    right, left = [first[0], late[1]], [late[0], first[1]]
    steps = (grid_size - 1) // 2
    for step in range(1, steps + 1):
        for h in (0, 1):
            right[h] = lax.ppermute(right[h], "grid", onward)
            left[1 - h] = lax.ppermute(left[1 - h], "grid", backward)
            pieces[(grid_size - step, h)] = right[h]
            pieces[(step, 1 - h)] = left[1 - h]
    last = {}
    if grid_size % 2 == 0:
        last[(steps + 1, 0)] = lax.ppermute(right[0], "grid", onward)
        last[(steps + 1, 1)] = lax.ppermute(left[1], "grid", backward)

    swapped = lax.ppermute(inner_tiles, "depth", [(0, 1), (1, 0)])
    inner = jnp.concatenate([inner_tiles, swapped], axis=0).reshape(-1, size, size)
    inner_mask, _ = lax.optimization_barrier((inner_mask, pieces[(grid_size - 1, 0)]))
    tile_flags = jnp.concatenate(
        [inner_mask, lax.ppermute(inner_mask, "depth", [(0, 1), (1, 0)])], axis=0
    )[:, 0]

    position = jnp.asarray(position_of, jnp.int32)[column]
    sources = jnp.asarray(order, jnp.int32)[
        (position + jnp.arange(grid_size, dtype=jnp.int32)) % grid_size
    ]
    true_column = held_col[sources]
    offset = true_column - column + local_offsets * halves // 2
    inside = (offset >= 0) & (offset < local_offsets * halves)
    offset = jnp.clip(offset, 0, local_offsets * halves - 1)
    band_row = lax.dynamic_index_in_dim(band_mask, depth_index, 0, keepdims=False)
    flags = jnp.where(inside, band_row[true_column], 0).astype(jnp.int32)
    slots = (
        jnp.where(offset // local_offsets == depth_index, 0, local_offsets)
        + offset % local_offsets
    ).astype(jnp.int32)

    flags = flags * tile_flags[slots]

    def placed(items):
        return [(source, h * half) for source, h in items]

    total_shape = jax.ShapeDtypeStruct((size, size), jnp.float32)
    early = multiply(
        early_kernel, placed(pieces), slots, flags, [inner, *pieces.values()], total_shape, []
    )
    tile = lax.dynamic_index_in_dim(inner, slots[steps + 1], 0, keepdims=False)
    tile = tile * flags[steps + 1].astype(tile.dtype)
    vmem = pl.BlockSpec(memory_space=pltpu.VMEM)
    return pl.pallas_call(
        late_kernel,
        out_shape=jax.ShapeDtypeStruct((size, size), band_held.dtype),
        in_specs=[vmem] * 4,
        out_specs=pl.BlockSpec(memory_space=pl.ANY),
        scratch_shapes=[
            pltpu.VMEM((size, size), band_held.dtype),
            pltpu.SemaphoreType.DMA((len(last),)),
        ],
        compiler_params=pltpu.CompilerParams(vmem_limit_bytes=40 * 2**20),
    )(tile, early, *last.values())


def per_device(band_held, inner_tiles, band_mask, inner_mask, held_col):
    window = inner_mask.shape[0] * lax.axis_size("depth")
    small = lax.axis_size("grid") <= 2 * window
    fits = lax.axis_size("depth") == 2 and band_mask.shape[0] == 2 and lax.axis_size("grid") % 2 == 0
    chosen = gather_columns if small and fits else exchange_columns
    return chosen(band_held, inner_tiles, band_mask, inner_mask, held_col)


def solution(mesh):
    placed = (
        P("groups", "grid"),
        P(("groups", "depth"), "grid"),
        P("groups", None),
        P(("groups", "depth"), "grid"),
        P("groups"),
    )
    return jax.shard_map(
        per_device,
        mesh=mesh,
        in_specs=placed,
        out_specs=P(("groups", "depth"), "grid"),
        check_vma=False,
    )
```

```python
import functools

import jax
import jax.numpy as jnp
from jax import lax
from jax.experimental import pallas as pl
from jax.experimental.pallas import tpu as pltpu
from jax.sharding import PartitionSpec as P


def exchange_columns(band_held, inner_tiles, band_mask, inner_mask, held_col):
    grid_size = lax.axis_size("grid")
    tile_size = band_held.shape[1]
    band_count = band_mask.shape[0]
    local_offsets = inner_mask.shape[0]
    depth_index = lax.axis_index("depth")
    column = lax.axis_index("grid")
    first_offset = depth_index * local_offsets
    right_flags = inner_mask[:, 0]
    row_count = band_count * tile_size
    col_order = jnp.arange(grid_size, dtype=jnp.int32)
    inverse = jnp.sum(
        jnp.where(held_col[None, :] == col_order[:, None], col_order[None, :], 0), axis=1
    )
    pieces = lax.all_to_all(
        band_held.reshape(row_count, 1, tile_size), "grid", split_axis=0, concat_axis=1, tiled=True
    )
    ordered = jnp.take(pieces, inverse, axis=1)
    padded = jnp.pad(ordered, ((0, 0), (local_offsets, local_offsets), (0, 0)))
    windows = jnp.stack(
        [
            lax.dynamic_slice_in_dim(padded, first_offset + offset, grid_size, 1)
            for offset in range(local_offsets)
        ],
        axis=2,
    )
    arrived = lax.all_to_all(windows, "grid", split_axis=1, concat_axis=0, tiled=True)
    arrived = arrived.reshape(row_count, local_offsets, tile_size)
    flags_pad = jnp.pad(band_mask, ((0, 0), (local_offsets, local_offsets)))
    keep_flags = (
        lax.dynamic_slice_in_dim(flags_pad, column + first_offset, local_offsets, 1)
        * right_flags[None, :]
    )
    keep_rows = jnp.repeat(keep_flags, tile_size, axis=0).astype(jnp.float32)
    summed = jnp.zeros((row_count, tile_size), jnp.float32)
    for offset in range(local_offsets):
        right_block = inner_tiles[offset * tile_size : (offset + 1) * tile_size]
        summed = (
            summed
            + jnp.dot(arrived[:, offset, :], right_block, preferred_element_type=jnp.float32)
            * keep_rows[:, offset : offset + 1]
        )
    summed = lax.psum_scatter(summed, "depth", scatter_dimension=0, tiled=True)
    return summed.astype(jnp.bfloat16)


def add_products(places, slots, flags, pieces, inner, total):
    for (source, row), piece in zip(places, pieces):
        rows = pl.ds(row, piece.shape[0])

        @pl.when(flags[source] != 0)
        def _():
            total[rows, :] += jnp.dot(
                piece[...], inner[slots[source]], preferred_element_type=jnp.float32
            )


def early_kernel(places, slots, flags, inner, *refs):
    total = refs[-1]
    total[...] = jnp.zeros_like(total)
    add_products(places, slots, flags, refs[:-1], inner, total)


def middle_kernel(places, last, slots, flags, inner, before, *refs):
    *pieces, total, late_flag, out, held, sem = refs
    late_flag[...] = jnp.full_like(late_flag, flags[last])
    total[...] = before[...]
    add_products(places, slots, flags, pieces, inner, total)
    held[...] = total[...].astype(held.dtype)
    copy = pltpu.make_async_copy(held, out, sem)
    copy.start()
    copy.wait()


def late_kernel(flag, tile, before, *refs):
    *pieces, _, out, held, sems = refs

    @pl.when(flag[0, 0] != 0)
    def _():
        copies = []
        start = 0
        for h, piece in enumerate(pieces):
            rows = pl.ds(start, piece.shape[0])
            start += piece.shape[0]
            product = jnp.dot(piece[...], tile[...], preferred_element_type=jnp.float32)
            held[rows, :] = (before[rows, :] + product).astype(out.dtype)
            copies.append(pltpu.make_async_copy(held.at[rows], out.at[rows], sems.at[h]))
            copies[-1].start()
        for copy in copies:
            copy.wait()


def gather_columns(band_held, inner_tiles, band_mask, inner_mask, held_col):
    grid_size = lax.axis_size("grid")
    size = band_held.shape[1]
    local_offsets = inner_mask.shape[0]
    halves = lax.axis_size("depth")
    depth_index = lax.axis_index("depth")
    column = lax.axis_index("grid")
    half = (size * 9 // 16) // 16 * 16

    order = list(range(0, grid_size, 2)) + list(range(1, grid_size, 2))[::-1]
    onward = [(order[i], order[(i + 1) % grid_size]) for i in range(grid_size)]
    backward = [(b, a) for a, b in onward]
    position_of = [order.index(g) for g in range(grid_size)]

    begin = depth_index * size
    again, _ = lax.optimization_barrier((band_held, inner_mask))
    first = [
        lax.dynamic_slice_in_dim(band_held, begin, half, 0),
        lax.dynamic_slice_in_dim(again, begin + half, size - half, 0),
    ]
    pieces = {(0, 0): first[0], (0, 1): first[1]}
    late = lax.optimization_barrier((*first, inner_mask))
    right, left = [first[0], late[1]], [late[0], first[1]]
    steps = (grid_size - 1) // 2
    for step in range(1, steps + 1):
        for h in (0, 1):
            right[h] = lax.ppermute(right[h], "grid", onward)
            left[1 - h] = lax.ppermute(left[1 - h], "grid", backward)
            pieces[(grid_size - step, h)] = right[h]
            pieces[(step, 1 - h)] = left[1 - h]
    last = {}
    if grid_size % 2 == 0:
        last[(steps + 1, 0)] = lax.ppermute(right[0], "grid", onward)
        last[(steps + 1, 1)] = lax.ppermute(left[1], "grid", backward)

    swapped = lax.ppermute(inner_tiles, "depth", [(0, 1), (1, 0)])
    inner = jnp.concatenate([inner_tiles, swapped], axis=0).reshape(-1, size, size)
    inner_mask, _ = lax.optimization_barrier((inner_mask, pieces[(grid_size - 1, 0)]))
    tile_flags = jnp.concatenate(
        [inner_mask, lax.ppermute(inner_mask, "depth", [(0, 1), (1, 0)])], axis=0
    )[:, 0]

    position = jnp.asarray(position_of, jnp.int32)[column]
    sources = jnp.asarray(order, jnp.int32)[
        (position + jnp.arange(grid_size, dtype=jnp.int32)) % grid_size
    ]
    true_column = held_col[sources]
    offset = true_column - column + local_offsets * halves // 2
    inside = (offset >= 0) & (offset < local_offsets * halves)
    offset = jnp.clip(offset, 0, local_offsets * halves - 1)
    band_row = lax.dynamic_index_in_dim(band_mask, depth_index, 0, keepdims=False)
    flags = jnp.where(inside, band_row[true_column], 0).astype(jnp.int32)
    slots = (
        jnp.where(offset // local_offsets == depth_index, 0, local_offsets)
        + offset % local_offsets
    ).astype(jnp.int32)

    flags = flags * tile_flags[slots]

    def placed(items):
        return [(source, h * half) for source, h in items]

    smem, vmem = pl.BlockSpec(memory_space=pltpu.SMEM), pl.BlockSpec(memory_space=pltpu.VMEM)
    anywhere = pl.BlockSpec(memory_space=pl.ANY)
    params = pltpu.CompilerParams(vmem_limit_bytes=40 * 2**20)
    result = jax.ShapeDtypeStruct((size, size), band_held.dtype)
    staged = pltpu.VMEM((size, size), band_held.dtype)
    wide = jax.ShapeDtypeStruct((size, size), jnp.float32)
    near = {k: x for k, x in pieces.items() if k[0] not in (steps, grid_size - steps)}
    far = {k: x for k, x in pieces.items() if k not in near}

    def cost(items):
        return pl.CostEstimate(
            flops=len(items) * size**3,
            bytes_accessed=2 * (inner.size + (len(items) + 2) * size**2),
            transcendentals=0,
        )

    early = pl.pallas_call(
        functools.partial(early_kernel, placed(near)),
        out_shape=wide,
        in_specs=[smem, smem] + [vmem] * (1 + len(near)),
        out_specs=vmem,
        compiler_params=params,
        cost_estimate=cost(near),
    )(slots, flags, inner, *near.values())
    total, late_flag, early = pl.pallas_call(
        functools.partial(middle_kernel, placed(far), steps + 1),
        out_shape=[wide, jax.ShapeDtypeStruct((8, 128), jnp.int32), result],
        in_specs=[smem, smem] + [vmem] * (2 + len(far)),
        out_specs=[vmem, vmem, anywhere],
        scratch_shapes=[staged, pltpu.SemaphoreType.DMA],
        compiler_params=params,
        cost_estimate=cost(far),
    )(slots, flags, inner, early, *far.values())
    tile = lax.dynamic_index_in_dim(inner, slots[steps + 1], 0, keepdims=False)
    return pl.pallas_call(
        late_kernel,
        out_shape=result,
        in_specs=[vmem] * (3 + len(last)) + [anywhere],
        out_specs=anywhere,
        scratch_shapes=[staged, pltpu.SemaphoreType.DMA((len(last),))],
        input_output_aliases={3 + len(last): 0},
        compiler_params=params,
    )(late_flag, tile, total, *last.values(), early)


def per_device(band_held, inner_tiles, band_mask, inner_mask, held_col):
    window = inner_mask.shape[0] * lax.axis_size("depth")
    small = lax.axis_size("grid") <= 2 * window
    fits = lax.axis_size("depth") == 2 and band_mask.shape[0] == 2 and lax.axis_size("grid") % 2 == 0
    chosen = gather_columns if small and fits else exchange_columns
    return chosen(band_held, inner_tiles, band_mask, inner_mask, held_col)


def solution(mesh):
    placed = (
        P("groups", "grid"),
        P(("groups", "depth"), "grid"),
        P("groups", None),
        P(("groups", "depth"), "grid"),
        P("groups"),
    )
    return jax.shard_map(
        per_device,
        mesh=mesh,
        in_specs=placed,
        out_specs=P(("groups", "depth"), "grid"),
        check_vma=False,
    )
```

```python
import functools

import jax
import jax.numpy as jnp
from jax import lax
from jax.experimental import pallas as pl
from jax.experimental.pallas import tpu as pltpu
from jax.sharding import PartitionSpec as P


def exchange_columns(band_held, inner_tiles, band_mask, inner_mask, held_col):
    grid_size = lax.axis_size("grid")
    tile_size = band_held.shape[1]
    band_count = band_mask.shape[0]
    local_offsets = inner_mask.shape[0]
    depth_index = lax.axis_index("depth")
    column = lax.axis_index("grid")
    first_offset = depth_index * local_offsets
    right_flags = inner_mask[:, 0]
    row_count = band_count * tile_size
    col_order = jnp.arange(grid_size, dtype=jnp.int32)
    inverse = jnp.sum(
        jnp.where(held_col[None, :] == col_order[:, None], col_order[None, :], 0), axis=1
    )
    pieces = lax.all_to_all(
        band_held.reshape(row_count, 1, tile_size), "grid", split_axis=0, concat_axis=1, tiled=True
    )
    ordered = jnp.take(pieces, inverse, axis=1)
    padded = jnp.pad(ordered, ((0, 0), (local_offsets, local_offsets), (0, 0)))
    windows = jnp.stack(
        [
            lax.dynamic_slice_in_dim(padded, first_offset + offset, grid_size, 1)
            for offset in range(local_offsets)
        ],
        axis=2,
    )
    arrived = lax.all_to_all(windows, "grid", split_axis=1, concat_axis=0, tiled=True)
    arrived = arrived.reshape(row_count, local_offsets, tile_size)
    flags_pad = jnp.pad(band_mask, ((0, 0), (local_offsets, local_offsets)))
    keep_flags = (
        lax.dynamic_slice_in_dim(flags_pad, column + first_offset, local_offsets, 1)
        * right_flags[None, :]
    )
    keep_rows = jnp.repeat(keep_flags, tile_size, axis=0).astype(jnp.float32)
    summed = jnp.zeros((row_count, tile_size), jnp.float32)
    for offset in range(local_offsets):
        right_block = inner_tiles[offset * tile_size : (offset + 1) * tile_size]
        summed = (
            summed
            + jnp.dot(arrived[:, offset, :], right_block, preferred_element_type=jnp.float32)
            * keep_rows[:, offset : offset + 1]
        )
    summed = lax.psum_scatter(summed, "depth", scatter_dimension=0, tiled=True)
    return summed.astype(jnp.bfloat16)


def add_products(places, slots, flags, pieces, inner, total):
    for (source, row), piece in zip(places, pieces):
        rows = pl.ds(row, piece.shape[0])

        @pl.when(flags[source] != 0)
        def _():
            total[rows, :] += jnp.dot(
                piece[...], inner[slots[source]], preferred_element_type=jnp.float32
            )


def early_kernel(places, slots, flags, inner, *refs):
    total = refs[-1]
    total[...] = jnp.zeros_like(total)
    add_products(places, slots, flags, refs[:-1], inner, total)


def middle_kernel(places, last, slots, flags, inner, before, *refs):
    *pieces, total, late_flag, out, held, sem = refs
    late_flag[...] = jnp.full_like(late_flag, flags[last])
    total[...] = before[...]
    add_products(places, slots, flags, pieces, inner, total)
    held[...] = total[...].astype(held.dtype)
    copy = pltpu.make_async_copy(held, out, sem)
    copy.start()
    copy.wait()


def late_kernel(flag, tile, before, *refs):
    *pieces, _, out, held, sems = refs

    @pl.when(flag[0, 0] != 0)
    def _():
        copies = []
        start = 0
        for h, piece in enumerate(pieces):
            rows = pl.ds(start, piece.shape[0])
            start += piece.shape[0]
            product = jnp.dot(piece[...], tile[...], preferred_element_type=jnp.float32)
            held[rows, :] = (before[rows, :] + product).astype(out.dtype)
            copies.append(pltpu.make_async_copy(held.at[rows], out.at[rows], sems.at[h]))
            copies[-1].start()
        for copy in copies:
            copy.wait()


def gather_columns(band_held, inner_tiles, band_mask, inner_mask, held_col):
    grid_size = lax.axis_size("grid")
    size = band_held.shape[1]
    local_offsets = inner_mask.shape[0]
    halves = lax.axis_size("depth")
    depth_index = lax.axis_index("depth")
    column = lax.axis_index("grid")
    half = (size * 9 // 16) // 16 * 16

    order = list(range(0, grid_size, 2)) + list(range(1, grid_size, 2))[::-1]
    onward = [(order[i], order[(i + 1) % grid_size]) for i in range(grid_size)]
    backward = [(b, a) for a, b in onward]
    position_of = [order.index(g) for g in range(grid_size)]

    begin = depth_index * size
    again, _ = lax.optimization_barrier((band_held, inner_mask))
    first = [
        lax.dynamic_slice_in_dim(band_held, begin, half, 0),
        lax.dynamic_slice_in_dim(again, begin + half, size - half, 0),
    ]
    pieces = {(0, 0): first[0], (0, 1): first[1]}
    late = lax.optimization_barrier((*first, inner_mask))
    right, left = [first[0], late[1]], [late[0], first[1]]
    steps = (grid_size - 1) // 2
    for step in range(1, steps + 1):
        for h in (0, 1):
            right[h] = lax.ppermute(right[h], "grid", onward)
            left[1 - h] = lax.ppermute(left[1 - h], "grid", backward)
            pieces[(grid_size - step, h)] = right[h]
            pieces[(step, 1 - h)] = left[1 - h]
    last = {}
    if grid_size % 2 == 0:
        last[(steps + 1, 0)] = lax.ppermute(right[0], "grid", onward)
        last[(steps + 1, 1)] = lax.ppermute(left[1], "grid", backward)

    swapped = lax.ppermute(inner_tiles, "depth", [(0, 1), (1, 0)])
    inner = jnp.concatenate([inner_tiles, swapped], axis=0).reshape(-1, size, size)
    inner_mask, _ = lax.optimization_barrier((inner_mask, pieces[(grid_size - 1, 1)]))
    tile_flags = jnp.concatenate(
        [inner_mask, lax.ppermute(inner_mask, "depth", [(0, 1), (1, 0)])], axis=0
    )[:, 0]

    position = jnp.asarray(position_of, jnp.int32)[column]
    sources = jnp.asarray(order, jnp.int32)[
        (position + jnp.arange(grid_size, dtype=jnp.int32)) % grid_size
    ]
    true_column = held_col[sources]
    offset = true_column - column + local_offsets * halves // 2
    inside = (offset >= 0) & (offset < local_offsets * halves)
    offset = jnp.clip(offset, 0, local_offsets * halves - 1)
    band_row = lax.dynamic_index_in_dim(band_mask, depth_index, 0, keepdims=False)
    flags = jnp.where(inside, band_row[true_column], 0).astype(jnp.int32)
    slots = (
        jnp.where(offset // local_offsets == depth_index, 0, local_offsets)
        + offset % local_offsets
    ).astype(jnp.int32)

    flags = flags * tile_flags[slots]

    def placed(items):
        return [(source, h * half) for source, h in items]

    smem, vmem = pl.BlockSpec(memory_space=pltpu.SMEM), pl.BlockSpec(memory_space=pltpu.VMEM)
    anywhere = pl.BlockSpec(memory_space=pl.ANY)
    params = pltpu.CompilerParams(vmem_limit_bytes=40 * 2**20)
    result = jax.ShapeDtypeStruct((size, size), band_held.dtype)
    staged = pltpu.VMEM((size, size), band_held.dtype)
    wide = jax.ShapeDtypeStruct((size, size), jnp.float32)
    near = {k: x for k, x in pieces.items() if k[0] not in (steps, grid_size - steps)}
    far = {k: x for k, x in pieces.items() if k not in near}

    def cost(items):
        return pl.CostEstimate(
            flops=3 * len(items) * size**3,
            bytes_accessed=2 * (inner.size + (len(items) + 2) * size**2),
            transcendentals=0,
        )

    early = pl.pallas_call(
        functools.partial(early_kernel, placed(near)),
        out_shape=wide,
        in_specs=[smem, smem] + [vmem] * (1 + len(near)),
        out_specs=vmem,
        compiler_params=params,
        cost_estimate=cost(near),
    )(slots, flags, inner, *near.values())
    total, late_flag, early = pl.pallas_call(
        functools.partial(middle_kernel, placed(far), steps + 1),
        out_shape=[wide, jax.ShapeDtypeStruct((8, 128), jnp.int32), result],
        in_specs=[smem, smem] + [vmem] * (2 + len(far)),
        out_specs=[vmem, vmem, anywhere],
        scratch_shapes=[staged, pltpu.SemaphoreType.DMA],
        compiler_params=params,
        cost_estimate=cost(far),
    )(slots, flags, inner, early, *far.values())
    tile = lax.dynamic_index_in_dim(inner, slots[steps + 1], 0, keepdims=False)
    return pl.pallas_call(
        late_kernel,
        out_shape=result,
        in_specs=[vmem] * (3 + len(last)) + [anywhere],
        out_specs=anywhere,
        scratch_shapes=[staged, pltpu.SemaphoreType.DMA((len(last),))],
        input_output_aliases={3 + len(last): 0},
        compiler_params=params,
    )(late_flag, tile, total, *last.values(), early)


def per_device(band_held, inner_tiles, band_mask, inner_mask, held_col):
    window = inner_mask.shape[0] * lax.axis_size("depth")
    small = lax.axis_size("grid") <= 2 * window
    fits = lax.axis_size("depth") == 2 and band_mask.shape[0] == 2 and lax.axis_size("grid") % 2 == 0
    chosen = gather_columns if small and fits else exchange_columns
    return chosen(band_held, inner_tiles, band_mask, inner_mask, held_col)


def solution(mesh):
    placed = (
        P("groups", "grid"),
        P(("groups", "depth"), "grid"),
        P("groups", None),
        P(("groups", "depth"), "grid"),
        P("groups"),
    )
    return jax.shard_map(
        per_device,
        mesh=mesh,
        in_specs=placed,
        out_specs=P(("groups", "depth"), "grid"),
        check_vma=False,
    )
```

```python
import functools

import jax
import jax.numpy as jnp
from jax import lax
from jax.experimental import pallas as pl
from jax.experimental.pallas import tpu as pltpu
from jax.sharding import PartitionSpec as P


def exchange_columns(band_held, inner_tiles, band_mask, inner_mask, held_col):
    grid_size = lax.axis_size("grid")
    tile_size = band_held.shape[1]
    band_count = band_mask.shape[0]
    local_offsets = inner_mask.shape[0]
    depth_index = lax.axis_index("depth")
    column = lax.axis_index("grid")
    first_offset = depth_index * local_offsets
    right_flags = inner_mask[:, 0]
    row_count = band_count * tile_size
    col_order = jnp.arange(grid_size, dtype=jnp.int32)
    inverse = jnp.sum(
        jnp.where(held_col[None, :] == col_order[:, None], col_order[None, :], 0), axis=1
    )
    pieces = lax.all_to_all(
        band_held.reshape(row_count, 1, tile_size), "grid", split_axis=0, concat_axis=1, tiled=True
    )
    ordered = jnp.take(pieces, inverse, axis=1)
    padded = jnp.pad(ordered, ((0, 0), (local_offsets, local_offsets), (0, 0)))
    windows = jnp.stack(
        [
            lax.dynamic_slice_in_dim(padded, first_offset + offset, grid_size, 1)
            for offset in range(local_offsets)
        ],
        axis=2,
    )
    arrived = lax.all_to_all(windows, "grid", split_axis=1, concat_axis=0, tiled=True)
    arrived = arrived.reshape(row_count, local_offsets, tile_size)
    flags_pad = jnp.pad(band_mask, ((0, 0), (local_offsets, local_offsets)))
    keep_flags = (
        lax.dynamic_slice_in_dim(flags_pad, column + first_offset, local_offsets, 1)
        * right_flags[None, :]
    )
    keep_rows = jnp.repeat(keep_flags, tile_size, axis=0).astype(jnp.float32)
    summed = jnp.zeros((row_count, tile_size), jnp.float32)
    for offset in range(local_offsets):
        right_block = inner_tiles[offset * tile_size : (offset + 1) * tile_size]
        summed = (
            summed
            + jnp.dot(arrived[:, offset, :], right_block, preferred_element_type=jnp.float32)
            * keep_rows[:, offset : offset + 1]
        )
    summed = lax.psum_scatter(summed, "depth", scatter_dimension=0, tiled=True)
    return summed.astype(jnp.bfloat16)


def add_products(places, slots, flags, pieces, inner, total):
    for (source, row), piece in zip(places, pieces):
        rows = pl.ds(row, piece.shape[0])

        @pl.when(flags[source] != 0)
        def _():
            total[rows, :] += jnp.dot(
                piece[...], inner[slots[source]], preferred_element_type=jnp.float32
            )


def early_kernel(places, slots, flags, inner, *refs):
    total = refs[-1]
    total[...] = jnp.zeros_like(total)
    add_products(places, slots, flags, refs[:-1], inner, total)


def middle_kernel(places, last, slots, flags, inner, before, *refs):
    *pieces, total, late_flag, out, held, sem = refs
    late_flag[...] = jnp.full_like(late_flag, flags[last])
    total[...] = before[...]
    add_products(places, slots, flags, pieces, inner, total)
    held[...] = total[...].astype(held.dtype)
    copy = pltpu.make_async_copy(held, out, sem)
    copy.start()
    copy.wait()


def late_kernel(flag, tile, before, *refs):
    *pieces, _, out, held, sems = refs

    @pl.when(flag[0, 0] != 0)
    def _():
        copies = []
        start = 0
        for h, piece in enumerate(pieces):
            rows = pl.ds(start, piece.shape[0])
            start += piece.shape[0]
            product = jnp.dot(piece[...], tile[...], preferred_element_type=jnp.float32)
            held[rows, :] = (before[rows, :] + product).astype(out.dtype)
            copies.append(pltpu.make_async_copy(held.at[rows], out.at[rows], sems.at[h]))
            copies[-1].start()
        for copy in copies:
            copy.wait()


def gather_columns(band_held, inner_tiles, band_mask, inner_mask, held_col):
    grid_size = lax.axis_size("grid")
    size = band_held.shape[1]
    local_offsets = inner_mask.shape[0]
    halves = lax.axis_size("depth")
    depth_index = lax.axis_index("depth")
    column = lax.axis_index("grid")
    half = (size * 9 // 16) // 16 * 16

    order = [0] + list(range(1, grid_size, 2)) + list(range(2, grid_size, 2))[::-1]
    onward = [(order[i], order[(i + 1) % grid_size]) for i in range(grid_size)]
    backward = [(b, a) for a, b in onward]
    position_of = [order.index(g) for g in range(grid_size)]

    begin = depth_index * size
    again, _ = lax.optimization_barrier((band_held, inner_mask))
    first = [
        lax.dynamic_slice_in_dim(band_held, begin, half, 0),
        lax.dynamic_slice_in_dim(again, begin + half, size - half, 0),
    ]
    pieces = {(0, 0): first[0], (0, 1): first[1]}
    late = lax.optimization_barrier((*first, inner_mask))
    right, left = [first[0], late[1]], [late[0], first[1]]
    steps = (grid_size - 1) // 2
    for step in range(1, steps + 1):
        for h in (0, 1):
            right[h] = lax.ppermute(right[h], "grid", onward)
            left[1 - h] = lax.ppermute(left[1 - h], "grid", backward)
            pieces[(grid_size - step, h)] = right[h]
            pieces[(step, 1 - h)] = left[1 - h]
    last = {}
    if grid_size % 2 == 0:
        last[(steps + 1, 0)] = lax.ppermute(right[0], "grid", onward)
        last[(steps + 1, 1)] = lax.ppermute(left[1], "grid", backward)

    swapped = lax.ppermute(inner_tiles, "depth", [(0, 1), (1, 0)])
    inner = jnp.concatenate([inner_tiles, swapped], axis=0).reshape(-1, size, size)
    inner_mask, _ = lax.optimization_barrier((inner_mask, pieces[(grid_size - 1, 1)]))
    tile_flags = jnp.concatenate(
        [inner_mask, lax.ppermute(inner_mask, "depth", [(0, 1), (1, 0)])], axis=0
    )[:, 0]

    position = jnp.asarray(position_of, jnp.int32)[column]
    sources = jnp.asarray(order, jnp.int32)[
        (position + jnp.arange(grid_size, dtype=jnp.int32)) % grid_size
    ]
    true_column = held_col[sources]
    offset = true_column - column + local_offsets * halves // 2
    inside = (offset >= 0) & (offset < local_offsets * halves)
    offset = jnp.clip(offset, 0, local_offsets * halves - 1)
    band_row = lax.dynamic_index_in_dim(band_mask, depth_index, 0, keepdims=False)
    flags = jnp.where(inside, band_row[true_column], 0).astype(jnp.int32)
    slots = (
        jnp.where(offset // local_offsets == depth_index, 0, local_offsets)
        + offset % local_offsets
    ).astype(jnp.int32)

    flags = flags * tile_flags[slots]

    def placed(items):
        return [(source, h * half) for source, h in items]

    smem, vmem = pl.BlockSpec(memory_space=pltpu.SMEM), pl.BlockSpec(memory_space=pltpu.VMEM)
    anywhere = pl.BlockSpec(memory_space=pl.ANY)
    params = pltpu.CompilerParams(vmem_limit_bytes=40 * 2**20)
    result = jax.ShapeDtypeStruct((size, size), band_held.dtype)
    staged = pltpu.VMEM((size, size), band_held.dtype)
    wide = jax.ShapeDtypeStruct((size, size), jnp.float32)
    near = {k: x for k, x in pieces.items() if k[0] not in (steps, grid_size - steps)}
    far = {k: x for k, x in pieces.items() if k not in near}

    def cost(items):
        return pl.CostEstimate(
            flops=3 * len(items) * size**3,
            bytes_accessed=2 * (inner.size + (len(items) + 2) * size**2),
            transcendentals=0,
        )

    early = pl.pallas_call(
        functools.partial(early_kernel, placed(near)),
        out_shape=wide,
        in_specs=[smem, smem] + [vmem] * (1 + len(near)),
        out_specs=vmem,
        compiler_params=params,
        cost_estimate=cost(near),
    )(slots, flags, inner, *near.values())
    total, late_flag, early = pl.pallas_call(
        functools.partial(middle_kernel, placed(far), steps + 1),
        out_shape=[wide, jax.ShapeDtypeStruct((8, 128), jnp.int32), result],
        in_specs=[smem, smem] + [vmem] * (2 + len(far)),
        out_specs=[vmem, vmem, anywhere],
        scratch_shapes=[staged, pltpu.SemaphoreType.DMA],
        compiler_params=params,
        cost_estimate=cost(far),
    )(slots, flags, inner, early, *far.values())
    tile = lax.dynamic_index_in_dim(inner, slots[steps + 1], 0, keepdims=False)
    return pl.pallas_call(
        late_kernel,
        out_shape=result,
        in_specs=[vmem] * (3 + len(last)) + [anywhere],
        out_specs=anywhere,
        scratch_shapes=[staged, pltpu.SemaphoreType.DMA((len(last),))],
        input_output_aliases={3 + len(last): 0},
        compiler_params=params,
    )(late_flag, tile, total, *last.values(), early)


def per_device(band_held, inner_tiles, band_mask, inner_mask, held_col):
    window = inner_mask.shape[0] * lax.axis_size("depth")
    small = lax.axis_size("grid") <= 2 * window
    fits = lax.axis_size("depth") == 2 and band_mask.shape[0] == 2 and lax.axis_size("grid") % 2 == 0
    chosen = gather_columns if small and fits else exchange_columns
    return chosen(band_held, inner_tiles, band_mask, inner_mask, held_col)


def solution(mesh):
    placed = (
        P("groups", "grid"),
        P(("groups", "depth"), "grid"),
        P("groups", None),
        P(("groups", "depth"), "grid"),
        P("groups"),
    )
    return jax.shard_map(
        per_device,
        mesh=mesh,
        in_specs=placed,
        out_specs=P(("groups", "depth"), "grid"),
        check_vma=False,
    )
```

```python
import functools

import jax
import jax.numpy as jnp
from jax import lax
from jax.experimental import pallas as pl
from jax.experimental.pallas import tpu as pltpu
from jax.sharding import PartitionSpec as P


def exchange_columns(band_held, inner_tiles, band_mask, inner_mask, held_col):
    grid_size = lax.axis_size("grid")
    tile_size = band_held.shape[1]
    band_count = band_mask.shape[0]
    local_offsets = inner_mask.shape[0]
    depth_index = lax.axis_index("depth")
    column = lax.axis_index("grid")
    first_offset = depth_index * local_offsets
    right_flags = inner_mask[:, 0]
    row_count = band_count * tile_size
    col_order = jnp.arange(grid_size, dtype=jnp.int32)
    inverse = jnp.sum(
        jnp.where(held_col[None, :] == col_order[:, None], col_order[None, :], 0), axis=1
    )
    pieces = lax.all_to_all(
        band_held.reshape(row_count, 1, tile_size), "grid", split_axis=0, concat_axis=1, tiled=True
    )
    ordered = jnp.take(pieces, inverse, axis=1)
    padded = jnp.pad(ordered, ((0, 0), (local_offsets, local_offsets), (0, 0)))
    windows = jnp.stack(
        [
            lax.dynamic_slice_in_dim(padded, first_offset + offset, grid_size, 1)
            for offset in range(local_offsets)
        ],
        axis=2,
    )
    arrived = lax.all_to_all(windows, "grid", split_axis=1, concat_axis=0, tiled=True)
    arrived = arrived.reshape(row_count, local_offsets, tile_size)
    flags_pad = jnp.pad(band_mask, ((0, 0), (local_offsets, local_offsets)))
    keep_flags = (
        lax.dynamic_slice_in_dim(flags_pad, column + first_offset, local_offsets, 1)
        * right_flags[None, :]
    )
    keep_rows = jnp.repeat(keep_flags, tile_size, axis=0).astype(jnp.float32)
    summed = jnp.zeros((row_count, tile_size), jnp.float32)
    for offset in range(local_offsets):
        right_block = inner_tiles[offset * tile_size : (offset + 1) * tile_size]
        summed = (
            summed
            + jnp.dot(arrived[:, offset, :], right_block, preferred_element_type=jnp.float32)
            * keep_rows[:, offset : offset + 1]
        )
    summed = lax.psum_scatter(summed, "depth", scatter_dimension=0, tiled=True)
    return summed.astype(jnp.bfloat16)


def add_products(places, slots, flags, pieces, inner, total):
    for (source, row), piece in zip(places, pieces):
        rows = pl.ds(row, piece.shape[0])

        @pl.when(flags[source] != 0)
        def _():
            total[rows, :] += jnp.dot(
                piece[...], inner[slots[source]], preferred_element_type=jnp.float32
            )


def early_kernel(places, slots, flags, inner, *refs):
    total = refs[-1]
    total[...] = jnp.zeros_like(total)
    add_products(places, slots, flags, refs[:-1], inner, total)


def middle_kernel(places, last, slots, flags, inner, before, *refs):
    *pieces, total, late_flag, out, held, sem = refs
    late_flag[...] = jnp.full_like(late_flag, flags[last])
    total[...] = before[...]
    add_products(places, slots, flags, pieces, inner, total)
    held[...] = total[...].astype(held.dtype)
    copy = pltpu.make_async_copy(held, out, sem)
    copy.start()
    copy.wait()


def late_kernel(flag, tile, before, *refs):
    *pieces, _, out, held, sems = refs

    @pl.when(flag[0, 0] != 0)
    def _():
        copies = []
        start = 0
        for h, piece in enumerate(pieces):
            rows = pl.ds(start, piece.shape[0])
            start += piece.shape[0]
            product = jnp.dot(piece[...], tile[...], preferred_element_type=jnp.float32)
            held[rows, :] = (before[rows, :] + product).astype(out.dtype)
            copies.append(pltpu.make_async_copy(held.at[rows], out.at[rows], sems.at[h]))
            copies[-1].start()
        for copy in copies:
            copy.wait()


def gather_columns(band_held, inner_tiles, band_mask, inner_mask, held_col):
    grid_size = lax.axis_size("grid")
    size = band_held.shape[1]
    local_offsets = inner_mask.shape[0]
    halves = lax.axis_size("depth")
    depth_index = lax.axis_index("depth")
    column = lax.axis_index("grid")
    half = (size * 19 // 32) // 16 * 16

    order = [0] + list(range(1, grid_size, 2)) + list(range(2, grid_size, 2))[::-1]
    onward = [(order[i], order[(i + 1) % grid_size]) for i in range(grid_size)]
    backward = [(b, a) for a, b in onward]
    position_of = [order.index(g) for g in range(grid_size)]

    begin = depth_index * size
    again, _ = lax.optimization_barrier((band_held, inner_mask))
    first = [
        lax.dynamic_slice_in_dim(band_held, begin, half, 0),
        lax.dynamic_slice_in_dim(again, begin + half, size - half, 0),
    ]
    pieces = {(0, 0): first[0], (0, 1): first[1]}
    late = lax.optimization_barrier((*first, inner_mask))
    right, left = [first[0], late[1]], [late[0], first[1]]
    steps = (grid_size - 1) // 2
    for step in range(1, steps + 1):
        for h in (0, 1):
            right[h] = lax.ppermute(right[h], "grid", onward)
            left[1 - h] = lax.ppermute(left[1 - h], "grid", backward)
            pieces[(grid_size - step, h)] = right[h]
            pieces[(step, 1 - h)] = left[1 - h]
    last = {}
    if grid_size % 2 == 0:
        last[(steps + 1, 0)] = lax.ppermute(right[0], "grid", onward)
        last[(steps + 1, 1)] = lax.ppermute(left[1], "grid", backward)

    swapped = lax.ppermute(inner_tiles, "depth", [(0, 1), (1, 0)])
    inner = jnp.concatenate([inner_tiles, swapped], axis=0).reshape(-1, size, size)
    inner_mask, _ = lax.optimization_barrier((inner_mask, pieces[(grid_size - 1, 1)]))
    tile_flags = jnp.concatenate(
        [inner_mask, lax.ppermute(inner_mask, "depth", [(0, 1), (1, 0)])], axis=0
    )[:, 0]

    position = jnp.asarray(position_of, jnp.int32)[column]
    sources = jnp.asarray(order, jnp.int32)[
        (position + jnp.arange(grid_size, dtype=jnp.int32)) % grid_size
    ]
    true_column = held_col[sources]
    offset = true_column - column + local_offsets * halves // 2
    inside = (offset >= 0) & (offset < local_offsets * halves)
    offset = jnp.clip(offset, 0, local_offsets * halves - 1)
    band_row = lax.dynamic_index_in_dim(band_mask, depth_index, 0, keepdims=False)
    flags = jnp.where(inside, band_row[true_column], 0).astype(jnp.int32)
    slots = (
        jnp.where(offset // local_offsets == depth_index, 0, local_offsets)
        + offset % local_offsets
    ).astype(jnp.int32)

    flags = flags * tile_flags[slots]

    def placed(items):
        return [(source, h * half) for source, h in items]

    smem, vmem = pl.BlockSpec(memory_space=pltpu.SMEM), pl.BlockSpec(memory_space=pltpu.VMEM)
    anywhere = pl.BlockSpec(memory_space=pl.ANY)
    params = pltpu.CompilerParams(vmem_limit_bytes=40 * 2**20)
    result = jax.ShapeDtypeStruct((size, size), band_held.dtype)
    staged = pltpu.VMEM((size, size), band_held.dtype)
    wide = jax.ShapeDtypeStruct((size, size), jnp.float32)
    near = {k: x for k, x in pieces.items() if k[0] not in (steps, grid_size - steps)}
    far = {k: x for k, x in pieces.items() if k not in near}

    def cost(items):
        return pl.CostEstimate(
            flops=3 * len(items) * size**3,
            bytes_accessed=2 * (inner.size + (len(items) + 2) * size**2),
            transcendentals=0,
        )

    early = pl.pallas_call(
        functools.partial(early_kernel, placed(near)),
        out_shape=wide,
        in_specs=[smem, smem] + [vmem] * (1 + len(near)),
        out_specs=vmem,
        compiler_params=params,
        cost_estimate=cost(near),
    )(slots, flags, inner, *near.values())
    total, late_flag, early = pl.pallas_call(
        functools.partial(middle_kernel, placed(far), steps + 1),
        out_shape=[wide, jax.ShapeDtypeStruct((8, 128), jnp.int32), result],
        in_specs=[smem, smem] + [vmem] * (2 + len(far)),
        out_specs=[vmem, vmem, anywhere],
        scratch_shapes=[staged, pltpu.SemaphoreType.DMA],
        compiler_params=params,
        cost_estimate=cost(far),
    )(slots, flags, inner, early, *far.values())
    tile = lax.dynamic_index_in_dim(inner, slots[steps + 1], 0, keepdims=False)
    return pl.pallas_call(
        late_kernel,
        out_shape=result,
        in_specs=[vmem] * (3 + len(last)) + [anywhere],
        out_specs=anywhere,
        scratch_shapes=[staged, pltpu.SemaphoreType.DMA((len(last),))],
        input_output_aliases={3 + len(last): 0},
        compiler_params=params,
    )(late_flag, tile, total, *last.values(), early)


def per_device(band_held, inner_tiles, band_mask, inner_mask, held_col):
    window = inner_mask.shape[0] * lax.axis_size("depth")
    small = lax.axis_size("grid") <= 2 * window
    fits = lax.axis_size("depth") == 2 and band_mask.shape[0] == 2 and lax.axis_size("grid") % 2 == 0
    chosen = gather_columns if small and fits else exchange_columns
    return chosen(band_held, inner_tiles, band_mask, inner_mask, held_col)


def solution(mesh):
    placed = (
        P("groups", "grid"),
        P(("groups", "depth"), "grid"),
        P("groups", None),
        P(("groups", "depth"), "grid"),
        P("groups"),
    )
    return jax.shard_map(
        per_device,
        mesh=mesh,
        in_specs=placed,
        out_specs=P(("groups", "depth"), "grid"),
        check_vma=False,
    )
```
